512 devices in a mesh: dom: 16 (over z, core), field: 32 (over y, x).
Axes of the slice: x: 4, y: 8, z: 8, core: 2. Of those that a mesh axis runs over, the one named last changes fastest.
Arguments:
- particles: bfloat16 [2048, 32768], P('dom', 'field'), may hold values from -12 to 12
- gradients: bfloat16 [2048, 32768], P('dom', 'field'), may hold values from -0.009765625 to 0.009765625
- kernel_scale: float32 [1], replicated, may hold values from 1966.08 to 2949.12
Outputs:
- velocity: float32 [2048, 32768], P('dom', 'field')
The draws below stay inside these ranges and needn't reach their ends.
All inputs are finite; a program needn't handle non-finite values.
Results may differ from the reference program's by a relative error of at most 0.0005.
Values may be sent and summed in bfloat16 or wider, within the bound.
No kernel may reach another device: no remote copies, remote signals or barrier semaphores. Data moves between devices by JAX's collectives and lax.ppermute only.
A program may use at most 64 MiB of HBM per device.

```python
import math
import jax
import jax.numpy as jnp
from jax import lax

C = 32768
PARTICLES = 2048


def draw_particles(key, part):
    key = jax.random.fold_in(key, 11)
    keys = jax.random.split(key, 7)
    column = jnp.arange(C) % 64
    marked = (jax.random.randint(keys[0], (C,), 0, 64) == 0).astype(jnp.float32)
    strong_level = jnp.exp(jax.random.uniform(keys[1], (C,), jnp.float32, math.log(1.6), math.log(4.0)))
    weak_level = jnp.exp(jax.random.uniform(keys[2], (C,), jnp.float32, math.log(0.08), math.log(0.3)))
    amplitude = marked * strong_level + (1.0 - marked) * weak_level
    factor = jax.random.normal(keys[3], (C,), jnp.float32)
    radius = jnp.exp(jax.random.uniform(keys[4], (PARTICLES, 1), jnp.float32, -0.35, 0.35))
    latent = jax.random.normal(keys[5], (PARTICLES, 64), jnp.float32)
    noise = jax.random.normal(keys[6], (PARTICLES, C), jnp.float32)
    values = radius * (0.2 * factor[None, :] * latent[:, column] + amplitude[None, :] * noise)
    values = jnp.clip(values, -12.0, 12.0)
    return values.astype(jnp.bfloat16)


def block_levels(key, dims, cuts, low, top_value):
    gain = 1.0
    for position, shards_of in cuts:
        steps = jax.random.uniform(jax.random.fold_in(jax.random.fold_in(key, 6), position), (shards_of,), jnp.float32, low / len(cuts), top_value / len(cuts))
        gain = gain * jnp.repeat(jnp.exp(steps), dims[position] // shards_of).reshape((-1,) + (1,) * (len(dims) - 1 - position))
    return gain


def bell_draw(rng, extent, scale, bound, cuts=(), kind=jnp.bfloat16):
    values = jax.random.normal(rng, extent, jnp.float32) * scale
    if len(cuts) > 0:
        values = block_levels(rng, extent, cuts, -0.22, 0.18) * values
    return jnp.clip(values, min=-bound, max=bound).astype(kind)


def setup_inputs(seed: int = 0) -> dict:
    streams_of = jax.random.split(jax.random.key(seed), 4)
    return {
        "particles": draw_particles(jax.random.fold_in(streams_of[3], 71), 0),
        "gradients": bell_draw(streams_of[1], (PARTICLES, C), (20.0 / C), 0.009765625, ((0, 16), (1, 32))),
        "kernel_scale": jnp.clip(jax.random.uniform(streams_of[2], (1,), jnp.float32, 1966.08, 2949.12), 1966.08, 2949.12),
    }


def reference(particles, gradients, kernel_scale):
    coords = particles.astype(jnp.float32)
    grads = gradients.astype(jnp.float32)
    norms = jnp.sum(coords * coords, axis=1)
    gram = jnp.dot(coords, coords.T, precision=lax.Precision.HIGHEST)
    dist = jnp.maximum(norms[:, None] + norms[None, :] - 2.0 * gram, 0.0)
    scale = kernel_scale[0]
    kernel = jnp.exp(-dist / scale).astype(jnp.bfloat16)
    kernel_wide = kernel.astype(jnp.float32)
    weight = jnp.sum(kernel_wide, axis=1)
    pulled = jnp.dot(kernel_wide, grads, precision=lax.Precision.HIGHEST)
    spread = jnp.dot(kernel_wide, coords, precision=lax.Precision.HIGHEST)
    return (0.5 * scale * pulled - spread + weight[:, None] * coords) / weight[:, None]
```

```python
import jax
import jax.numpy as jnp
from jax import lax
from jax.sharding import Mesh, PartitionSpec as P

DOM = ("z", "core")
FIELD = ("y", "x")
NF = 32


def dot_rows(left, right):
    return lax.dot_general(
        left, right, (((1,), (1,)), ((), ())), preferred_element_type=jnp.float32
    )


def squares_of(block):
    wide = block.astype(jnp.float32)
    return jnp.sum(wide * wide, axis=1)


def on_device(particles, gradients, kernel_scale):
    scale = kernel_scale[0]
    all_coords = lax.all_gather(particles, DOM, axis=0, tiled=True)
    all_grads = lax.all_gather(gradients, DOM, axis=0, tiled=True)
    partial = (
        squares_of(particles)[:, None]
        + squares_of(all_coords)[None, :]
        - 2.0 * dot_rows(particles, all_coords)
    ).astype(jnp.bfloat16)
    slots = partial.reshape(2, 64, 16, 128).transpose(2, 0, 1, 3).reshape(NF, 64, 128)
    terms = lax.all_to_all(slots, FIELD, 0, 0, tiled=True)
    dist = jnp.maximum(jnp.sum(terms.astype(jnp.float32), axis=0), 0.0)
    piece = jnp.exp(-dist / scale).astype(jnp.bfloat16)
    pieces = lax.all_to_all(
        jnp.broadcast_to(piece[None], (NF, 64, 128)), FIELD, 0, 0, tiled=True
    )
    kernel = pieces.reshape(16, 2, 64, 128).transpose(1, 2, 0, 3).reshape(128, 2048)
    weight = jnp.sum(kernel.astype(jnp.float32), axis=1)
    pulled = jnp.dot(kernel, all_grads, preferred_element_type=jnp.float32)
    spread = jnp.dot(kernel, all_coords, preferred_element_type=jnp.float32)
    coords = particles.astype(jnp.float32)
    return (0.5 * scale * pulled - spread + weight[:, None] * coords) / weight[:, None]


def solution(mesh):
    fine = Mesh(mesh.devices.reshape(8, 2, 8, 4), DOM + FIELD)
    placed = (P(DOM, FIELD), P(DOM, FIELD), P())
    return jax.shard_map(
        on_device, mesh=fine, in_specs=placed, out_specs=P(DOM, FIELD), check_vma=False
    )
```

```python
import jax
import jax.numpy as jnp
import numpy as np
from jax import lax
from jax.experimental import pallas as pl
from jax.experimental.pallas import tpu as pltpu
from jax.sharding import Mesh, PartitionSpec as P

DOM = ("z", "core")
FIELD = ("y", "x")
NZ, NC, NY, NX = 8, 2, 8, 4
NF = NY * NX
ROWS, COLS = 128, 1024
VMEM = 48 * 1024 * 1024
OFFSETS = (0, -1, -2, 2, 1, 3, 4, -3)


def dot_rows(left, right):
    return lax.dot_general(
        left, right, (((1,), (1,)), ((), ())), preferred_element_type=jnp.float32
    )


def shift(array, hops):
    return lax.ppermute(array, "z", [(i, (i + hops) % NZ) for i in range(NZ)])


def other_core(array):
    return lax.ppermute(array, "core", [(0, 1), (1, 0)])


def partial_body(a0, b0, a1, b1, a2, b2, a3, b3, out):
    blocks = [ref[...] for ref in (a0, b0, a1, b1, a2, b2, a3, b3)]
    ones = jnp.ones((ROWS, COLS), jnp.bfloat16)
    high, low = [], []
    for block in blocks:
        wide = block.astype(jnp.float32)
        square = wide * wide
        top = square.astype(jnp.bfloat16)
        high.append(top)
        low.append((square - top.astype(jnp.float32)).astype(jnp.bfloat16))

    def along_lanes(i):
        return dot_rows(ones[:8], high[i]) + dot_rows(ones[:8], low[i])

    def along_rows(i):
        return dot_rows(high[i], ones) + dot_rows(low[i], ones)

    lanes = [along_lanes(i)[0:1] for i in range(8)]
    for row, first, columns in ((0, 0, range(8)), (2, 16, (0, 1, 6, 7)), (6, 24, (4, 5, 2, 3))):
        norms = along_rows(row)
        for j, col in enumerate(columns):
            gram = dot_rows(blocks[row], blocks[col])
            part = (norms + lanes[col] - 2.0 * gram).astype(jnp.bfloat16)
            block = first + (j // 2) * 4 + j % 2
            out[block] = part[:64]
            out[block + 2] = part[64:]


def partial_distances(*blocks):
    return pl.pallas_call(
        partial_body,
        out_shape=jax.ShapeDtypeStruct((NF, 64, 128), jnp.bfloat16),
        in_specs=[pl.BlockSpec(memory_space=pltpu.VMEM)] * 8,
        out_specs=pl.BlockSpec(memory_space=pltpu.VMEM),
        compiler_params=pltpu.CompilerParams(vmem_limit_bytes=VMEM),
        cost_estimate=pl.CostEstimate(
            flops=2 * 24 * ROWS * ROWS * COLS, bytes_accessed=5 << 19, transcendentals=0
        ),
    )(*blocks)


def update_body(place, scale, slots, both, coords, out, pulled, spread, weight):
    step = pl.program_id(0)

    @pl.when(step == 0)
    def _():
        pulled[...] = jnp.zeros_like(pulled)
        spread[...] = jnp.zeros_like(spread)
        weight[...] = jnp.zeros_like(weight)

    same = jnp.concatenate([slots[0], slots[2]], axis=0)
    other = jnp.concatenate([slots[1], slots[3]], axis=0)
    swapped = place[NZ] == 1
    kernel = jnp.concatenate(
        [jnp.where(swapped, other, same), jnp.where(swapped, same, other)], axis=1
    )
    xs = jnp.concatenate([both[0, 0:128], both[0, 256:384]], axis=0)
    gs = jnp.concatenate([both[0, 128:256], both[0, 384:512]], axis=0)
    pulled[...] += jnp.dot(kernel, gs, preferred_element_type=jnp.float32)
    spread[...] += jnp.dot(kernel, xs, preferred_element_type=jnp.float32)
    weight[...] += jnp.sum(kernel.astype(jnp.float32), axis=1, keepdims=True)

    @pl.when(step == NZ - 1)
    def _():
        total = weight[...]
        out[...] = (
            (0.5 * scale[0]) * pulled[...]
            - spread[...]
            + total * coords[...].astype(jnp.float32)
        ) / total


def update(place, scale, slots, both, coords):
    return pl.pallas_call(
        update_body,
        out_shape=jax.ShapeDtypeStruct((ROWS, COLS), jnp.float32),
        grid_spec=pltpu.PrefetchScalarGridSpec(
            num_scalar_prefetch=2,
            grid=(NZ,),
            in_specs=[
                pl.BlockSpec((4, 64, 128), lambda k, place, scale: (k, 0, 0)),
                pl.BlockSpec((1, 512, COLS), lambda k, place, scale: (place[k], 0, 0)),
                pl.BlockSpec((ROWS, COLS), lambda k, place, scale: (0, 0)),
            ],
            out_specs=pl.BlockSpec((ROWS, COLS), lambda k, place, scale: (0, 0)),
            scratch_shapes=[
                pltpu.VMEM((ROWS, COLS), jnp.float32),
                pltpu.VMEM((ROWS, COLS), jnp.float32),
                pltpu.VMEM((ROWS, 1), jnp.float32),
            ],
        ),
        compiler_params=pltpu.CompilerParams(vmem_limit_bytes=VMEM),
        cost_estimate=pl.CostEstimate(
            flops=4 * ROWS * 2048 * COLS, bytes_accessed=10 << 20, transcendentals=0
        ),
    )(place, scale, slots, both, coords)


def homeward():
    pairs = []
    for z in range(NZ):
        for field in range(NF):
            hops = 0 if field < 16 else (-1 if field < 24 else 2)
            pairs.append((z * NF + field, (z + hops) % NZ * NF + field))
    return pairs


def on_device(particles, gradients, kernel_scale):
    z, core = lax.axis_index("z"), lax.axis_index("core")
    place = jnp.concatenate(
        [(z + np.array(OFFSETS, np.int32) + NZ) % NZ, core[None]]
    ).astype(jnp.int32)
    both = lax.all_gather(jnp.concatenate([particles, gradients], axis=0), DOM, axis=0, tiled=True)
    a1 = shift(particles, 1)
    a2 = shift(particles, 2)
    a3 = shift(particles, -2)
    b0 = other_core(particles)
    b1, b2, b3 = other_core(a1), other_core(a2), other_core(a3)
    slots = partial_distances(particles, b0, a1, b1, a2, b2, a3, b3)
    terms = lax.all_to_all(slots, FIELD, 0, 0, tiled=True)
    dist = jnp.maximum(jnp.sum(terms.astype(jnp.float32), axis=0), 0.0)
    piece = jnp.exp(-dist / kernel_scale[0]).astype(jnp.bfloat16)
    piece = lax.ppermute(piece, ("z",) + FIELD, homeward())
    pieces = lax.all_to_all(
        jnp.broadcast_to(piece[None], (NF, 64, 128)), FIELD, 0, 0, tiled=True
    )
    return update(place, kernel_scale, pieces, both.reshape(NZ, 512, COLS), particles)


def solution(mesh):
    fine = Mesh(mesh.devices.reshape(NZ, NC, NY, NX), DOM + FIELD)
    placed = (P(DOM, FIELD), P(DOM, FIELD), P())
    return jax.shard_map(
        on_device, mesh=fine, in_specs=placed, out_specs=P(DOM, FIELD), check_vma=False
    )
```

```python
import jax
import jax.numpy as jnp
import numpy as np
from jax import lax
from jax.experimental import pallas as pl
from jax.experimental.pallas import tpu as pltpu
from jax.sharding import Mesh, PartitionSpec as P

DOM = ("z", "core")
FIELD = ("y", "x")
NZ, NC, NY, NX = 8, 2, 8, 4
NF = NY * NX
ROWS, COLS = 128, 1024
VMEM = 48 * 1024 * 1024
OFFSETS = (0, -1, -2, 2, 1, 3, 4, -3)


def dot_rows(left, right):
    return lax.dot_general(
        left, right, (((1,), (1,)), ((), ())), preferred_element_type=jnp.float32
    )


def shift(array, hops):
    return lax.ppermute(array, "z", [(i, (i + hops) % NZ) for i in range(NZ)])


def other_core(array):
    return lax.ppermute(array, "core", [(0, 1), (1, 0)])


def partial_body(source, b0, a1, b1, far, far_b, out, a0, arrived):
    copy = pltpu.make_async_copy(source, a0, arrived)
    copy.start()
    copy.wait()
    blocks = [ref[...] for ref in (a0, b0, a1, b1)]
    blocks += [far[:ROWS], far_b[:ROWS], far[ROWS:], far_b[ROWS:]]
    ones = jnp.ones((ROWS, COLS), jnp.bfloat16)
    high, low = [], []
    for block in blocks:
        wide = block.astype(jnp.float32)
        square = wide * wide
        top = square.astype(jnp.bfloat16)
        high.append(top)
        low.append((square - top.astype(jnp.float32)).astype(jnp.bfloat16))

    def along_lanes(i):
        return dot_rows(ones[:8], high[i]) + dot_rows(ones[:8], low[i])

    def along_rows(i):
        return dot_rows(high[i], ones) + dot_rows(low[i], ones)

    lanes = [along_lanes(i)[0:1] for i in range(8)]
    for row, first, columns in ((0, 0, range(8)), (2, 16, (0, 1, 6, 7)), (6, 24, (4, 5, 2, 3))):
        norms = along_rows(row)
        for j, col in enumerate(columns):
            gram = dot_rows(blocks[row], blocks[col])
            part = (norms + lanes[col] - 2.0 * gram).astype(jnp.bfloat16)
            block = first + (j // 2) * 4 + j % 2
            out[block] = part[:64]
            out[block + 2] = part[64:]


def partial_distances(*blocks):
    return pl.pallas_call(
        partial_body,
        out_shape=jax.ShapeDtypeStruct((NF, 64, 128), jnp.bfloat16),
        in_specs=[pl.BlockSpec(memory_space=pltpu.HBM)]
        + [pl.BlockSpec(memory_space=pltpu.VMEM)] * 5,
        out_specs=pl.BlockSpec(memory_space=pltpu.VMEM),
        scratch_shapes=[pltpu.VMEM((ROWS, COLS), jnp.bfloat16), pltpu.SemaphoreType.DMA],
        compiler_params=pltpu.CompilerParams(vmem_limit_bytes=VMEM),
        cost_estimate=pl.CostEstimate(
            flops=2 * 24 * ROWS * ROWS * COLS, bytes_accessed=5 << 19, transcendentals=0
        ),
    )(*blocks)


def update_body(place, half, slots, both, out, kernel, weight):
    core = place[NZ]

    @pl.when(pl.program_id(0) == 0)
    def _():
        total = jnp.zeros((ROWS, 1), jnp.float32)
        for k in range(NZ):
            same = jnp.concatenate([slots[4 * k], slots[4 * k + 2]], axis=0)
            other = jnp.concatenate([slots[4 * k + 1], slots[4 * k + 3]], axis=0)
            pair = jnp.concatenate(
                [jnp.where(core == 1, other, same), jnp.where(core == 1, same, other)], axis=1
            )
            kernel[:, pl.ds(pl.multiple_of(place[k] * 256, 256), 256)] = pair
            total += jnp.sum(pair.astype(jnp.float32), axis=1, keepdims=True)
        weight[...] = total

    coords = jnp.concatenate([both[2 * d] for d in range(NZ * NC)], axis=0)
    grads = jnp.concatenate([both[2 * d + 1] for d in range(NZ * NC)], axis=0)
    pulled = jnp.dot(kernel[...], grads, preferred_element_type=jnp.float32)
    spread = jnp.dot(kernel[...], coords, preferred_element_type=jnp.float32)
    own = both[4 * place[0] + 2 * core].astype(jnp.float32)
    total = weight[...]
    out[...] = (half[0] * pulled - spread + total * own) / total


def update(place, half, slots, both):
    tile = 256
    return pl.pallas_call(
        update_body,
        out_shape=jax.ShapeDtypeStruct((ROWS, COLS), jnp.float32),
        grid_spec=pltpu.PrefetchScalarGridSpec(
            num_scalar_prefetch=2,
            grid=(COLS // tile,),
            in_specs=[
                pl.BlockSpec((NF, 64, 128), lambda k, place, half: (0, 0, 0)),
                pl.BlockSpec((2 * NZ * NC, ROWS, tile), lambda k, place, half: (0, 0, k)),
            ],
            out_specs=pl.BlockSpec((ROWS, tile), lambda k, place, half: (0, k)),
            scratch_shapes=[
                pltpu.VMEM((ROWS, 2048), jnp.bfloat16),
                pltpu.VMEM((ROWS, 1), jnp.float32),
            ],
        ),
        compiler_params=pltpu.CompilerParams(vmem_limit_bytes=VMEM),
        cost_estimate=pl.CostEstimate(
            flops=4 * ROWS * 2048 * COLS, bytes_accessed=10 << 20, transcendentals=0
        ),
    )(place, half, slots, both)


def homeward():
    pairs = []
    for z in range(NZ):
        for field in range(NF):
            hops = 0 if field < 16 else (-1 if field < 24 else 2)
            pairs.append((z * NF + field, (z + hops) % NZ * NF + field))
    return pairs


def on_device(particles, gradients, kernel_scale):
    z, core = lax.axis_index("z"), lax.axis_index("core")
    place = jnp.concatenate(
        [(z + np.array(OFFSETS, np.int32) + NZ) % NZ, core[None]]
    ).astype(jnp.int32)
    half = 0.5 * kernel_scale
    a1, a3 = shift(particles, 1), shift(particles, -2)
    b0 = other_core(particles)
    a1, b0 = lax.optimization_barrier((a1, b0))
    a2 = shift(a1, 1)
    b1 = other_core(a1)
    far = jnp.concatenate([a2, a3], axis=0)
    own = jnp.concatenate([particles, gradients], axis=0)
    own, far = lax.optimization_barrier((own, far))
    both = lax.all_gather(own, DOM, axis=0, tiled=True)
    slots = partial_distances(particles, b0, a1, b1, far, other_core(far))
    slots, place, half, whole = lax.optimization_barrier((slots, place, half, 2.0 * half))
    terms = lax.all_to_all(slots, FIELD, 0, 0, tiled=True)
    dist = jnp.maximum(jnp.sum(terms.astype(jnp.float32), axis=0), 0.0)
    piece = jnp.exp(-dist / whole[0]).astype(jnp.bfloat16)
    piece = lax.ppermute(piece, ("z",) + FIELD, homeward())
    pieces = lax.all_to_all(
        jnp.broadcast_to(piece[None], (NF, 64, 128)), FIELD, 0, 0, tiled=True
    )
    return update(place, half, pieces, both.reshape(2 * NZ * NC, ROWS, COLS))


def solution(mesh):
    fine = Mesh(mesh.devices.reshape(NZ, NC, NY, NX), DOM + FIELD)
    placed = (P(DOM, FIELD), P(DOM, FIELD), P())
    return jax.shard_map(
        on_device, mesh=fine, in_specs=placed, out_specs=P(DOM, FIELD), check_vma=False
    )
```

```python
import jax
import jax.numpy as jnp
import numpy as np
from jax import lax
from jax.experimental import pallas as pl
from jax.experimental.pallas import tpu as pltpu
from jax.sharding import Mesh, PartitionSpec as P

DOM = ("z", "core")
FIELD = ("y", "x")
NZ, NC, NY, NX = 8, 2, 8, 4
NF = NY * NX
ROWS, COLS = 128, 1024
VMEM = 48 * 1024 * 1024
OFFSETS = (0, -1, -2, 2, 1, 3, 4, -3)


def dot_rows(left, right):
    return lax.dot_general(
        left, right, (((1,), (1,)), ((), ())), preferred_element_type=jnp.float32
    )


def shift(array, hops):
    return lax.ppermute(array, "z", [(i, (i + hops) % NZ) for i in range(NZ)])


def other_core(array):
    return lax.ppermute(array, "core", [(0, 1), (1, 0)])


def partial_body(a1, b1, far, far_b, out, held, arrived):
    rows = [pl.ds(i * ROWS, ROWS) for i in range(3)]
    sources = (far.at[rows[0]], far_b.at[rows[0]], a1, b1)
    sources += (far.at[rows[1]], far_b.at[rows[1]], far.at[rows[2]], far_b.at[rows[2]])
    copies = [
        pltpu.make_async_copy(source, held.at[i], arrived.at[i])
        for i, source in enumerate(sources)
    ]
    for copy in copies:
        copy.start()
    for copy in copies:
        copy.wait()
    ones = jnp.ones((8, COLS), jnp.bfloat16)
    norms, lanes = {}, {}
    for i in range(8):
        wide = held[i].astype(jnp.float32)
        square = wide * wide
        if i in (0, 2, 6):
            norms[i] = jnp.sum(square, axis=1, keepdims=True)
        top = square.astype(jnp.bfloat16)
        rest = (square - top.astype(jnp.float32)).astype(jnp.bfloat16)
        lanes[i] = (dot_rows(ones, top) + dot_rows(ones, rest))[0:1]
    for row, first, columns in ((0, 0, range(8)), (2, 16, (0, 1, 6, 7)), (6, 24, (4, 5, 2, 3))):
        for j, col in enumerate(columns):
            gram = dot_rows(held[row], held[col])
            part = (norms[row] + lanes[col] - 2.0 * gram).astype(jnp.bfloat16)
            block = first + (j // 2) * 4 + j % 2
            out[block] = part[:64]
            out[block + 2] = part[64:]


def partial_distances(*blocks):
    return pl.pallas_call(
        partial_body,
        out_shape=jax.ShapeDtypeStruct((NF, 64, 128), jnp.bfloat16),
        in_specs=[pl.BlockSpec(memory_space=pl.ANY)] * 4,
        out_specs=pl.BlockSpec(memory_space=pltpu.VMEM),
        scratch_shapes=[
            pltpu.VMEM((8, ROWS, COLS), jnp.bfloat16),
            pltpu.SemaphoreType.DMA((8,)),
        ],
        compiler_params=pltpu.CompilerParams(vmem_limit_bytes=VMEM),
        cost_estimate=pl.CostEstimate(
            flops=2 * 24 * ROWS * ROWS * COLS, bytes_accessed=5 << 19, transcendentals=0
        ),
    )(*blocks)


def update_body(place, half, slots, both, out, xs, gs, arrived):
    copies = [
        [
            pltpu.make_async_copy(
                both.at[place[i] + kind], held.at[i * ROWS : (i + 1) * ROWS], arrived.at[kind, i]
            )
            for i in range(NZ * NC)
        ]
        for kind, held in enumerate((xs, gs))
    ]
    for copy in copies[0] + copies[1]:
        copy.start()
    blocks = []
    for k in range(NZ):
        blocks.append(jnp.concatenate([slots[4 * k], slots[4 * k + 2]], axis=0))
        blocks.append(jnp.concatenate([slots[4 * k + 1], slots[4 * k + 3]], axis=0))
    kernel = jnp.concatenate(blocks, axis=1)
    weight = jnp.sum(kernel.astype(jnp.float32), axis=1, keepdims=True)
    tiles = [slice(start, start + 256) for start in range(0, COLS, 256)]
    middle = NZ * NC // 2
    for copy in copies[0][:middle]:
        copy.wait()
    first, second = slice(0, middle * ROWS), slice(middle * ROWS, None)
    for at in tiles:
        spread = jnp.dot(kernel[:, first], xs[first, at], preferred_element_type=jnp.float32)
        out[:, at] = weight * xs[:ROWS, at].astype(jnp.float32) - spread
    for copy in copies[0][middle:]:
        copy.wait()
    for at in tiles:
        out[:, at] -= jnp.dot(kernel[:, second], xs[second, at], preferred_element_type=jnp.float32)
    for copy in copies[1]:
        copy.wait()
    for at in tiles:
        pulled = jnp.dot(kernel, gs[:, at], preferred_element_type=jnp.float32)
        out[:, at] = (half[0] * pulled + out[:, at]) / weight


def update(place, half, slots, both):
    return pl.pallas_call(
        update_body,
        out_shape=jax.ShapeDtypeStruct((ROWS, COLS), jnp.float32),
        in_specs=[
            pl.BlockSpec(memory_space=pltpu.SMEM),
            pl.BlockSpec(memory_space=pltpu.SMEM),
            pl.BlockSpec(memory_space=pltpu.VMEM),
            pl.BlockSpec(memory_space=pl.ANY),
        ],
        out_specs=pl.BlockSpec(memory_space=pltpu.VMEM),
        scratch_shapes=[
            pltpu.VMEM((2048, COLS), jnp.bfloat16),
            pltpu.VMEM((2048, COLS), jnp.bfloat16),
            pltpu.SemaphoreType.DMA((2, NZ * NC)),
        ],
        compiler_params=pltpu.CompilerParams(vmem_limit_bytes=VMEM),
        cost_estimate=pl.CostEstimate(
            flops=4 * ROWS * 2048 * COLS, bytes_accessed=10 << 20, transcendentals=0
        ),
    )(place, half, slots, both)


def homeward():
    pairs = []
    for z in range(NZ):
        for field in range(NF):
            hops = 0 if field < 16 else (-1 if field < 24 else 2)
            pairs.append((z * NF + field, (z + hops) % NZ * NF + field))
    return pairs


def on_device(particles, gradients, kernel_scale):
    z, core = lax.axis_index("z"), lax.axis_index("core")
    index = np.arange(NZ * NC)
    chips = (z + np.array(OFFSETS, np.int32)[index // 2] + NZ) % NZ
    place = (4 * chips + 2 * ((core + index % 2) % 2)).astype(jnp.int32)
    half = 0.5 * kernel_scale
    own = jnp.concatenate([particles, gradients], axis=0)
    a1, a3 = shift(particles, 1), shift(particles, -2)
    a2 = shift(a1, 1)
    b1 = other_core(a1)
    far = jnp.concatenate([particles, a2, a3], axis=0)
    far, b1, own, place, half, whole = lax.optimization_barrier(
        (far, b1, own, place, half, 2.0 * half)
    )
    both = lax.all_gather(own, DOM, axis=0, tiled=True)
    slots = partial_distances(a1, b1, far, other_core(far))
    terms = lax.all_to_all(slots, FIELD, 0, 0, tiled=True)
    dist = jnp.maximum(jnp.sum(terms.astype(jnp.float32), axis=0), 0.0)
    piece = jnp.exp(-dist / whole[0]).astype(jnp.bfloat16)
    piece = lax.ppermute(piece, ("z",) + FIELD, homeward())
    pieces = lax.all_to_all(
        jnp.broadcast_to(piece[None], (NF, 64, 128)), FIELD, 0, 0, tiled=True
    )
    return update(place, half, pieces, both.reshape(2 * NZ * NC, ROWS, COLS))


def solution(mesh):
    fine = Mesh(mesh.devices.reshape(NZ, NC, NY, NX), DOM + FIELD)
    placed = (P(DOM, FIELD), P(DOM, FIELD), P())
    return jax.shard_map(
        on_device, mesh=fine, in_specs=placed, out_specs=P(DOM, FIELD), check_vma=False
    )
```

```python
import jax
import jax.numpy as jnp
import numpy as np
from jax import lax
from jax.experimental import pallas as pl
from jax.experimental.pallas import tpu as pltpu
from jax.sharding import Mesh, PartitionSpec as P

DOM = ("z", "core")
FIELD = ("y", "x")
NZ, NC, NY, NX = 8, 2, 8, 4
NF = NY * NX
ROWS, COLS = 128, 1024
VMEM = 48 * 1024 * 1024
OFFSETS = (0, -1, -2, 2, 1, 3, 4, -3)


def dot_rows(left, right):
    return lax.dot_general(
        left, right, (((1,), (1,)), ((), ())), preferred_element_type=jnp.float32
    )


def shift(array, hops):
    return lax.ppermute(array, "z", [(i, (i + hops) % NZ) for i in range(NZ)])


def other_core(array):
    return lax.ppermute(array, "core", [(0, 1), (1, 0)])


def partial_body(a, b, a2, out, held, arrived):
    rows = [pl.ds(i * ROWS, ROWS) for i in range(3)]
    sources = [ref.at[at] for at in rows for ref in (a, b)] + [a2]
    copies = [
        pltpu.make_async_copy(source, held.at[i], arrived.at[i])
        for i, source in enumerate(sources)
    ]
    for copy in copies:
        copy.start()
    for copy in copies:
        copy.wait()
    ones = jnp.ones((8, COLS), jnp.bfloat16)
    norms, lanes = {}, {}
    for i in range(7):
        wide = held[i].astype(jnp.float32)
        square = wide * wide
        if i < 6:
            norms[i] = jnp.sum(square, axis=1, keepdims=True)
        if i % 2 == 0:
            top = square.astype(jnp.bfloat16)
            rest = (square - top.astype(jnp.float32)).astype(jnp.bfloat16)
            lanes[i] = (dot_rows(ones, top) + dot_rows(ones, rest))[0:1]
    for first, pairs in (
        (0, ((0, 0), (1, 2), (2, 6), (3, 4))),
        (2, ((4, 0), (5, 4))),
        (4, ((6, 6), (7, 2))),
    ):
        for r in range(NC):
            for k, col in pairs:
                gram = dot_rows(held[first + r], held[col])
                part = (norms[first + r] + lanes[col] - 2.0 * gram).astype(jnp.bfloat16)
                out[4 * k + r] = part[:64]
                out[4 * k + 2 + r] = part[64:]


def partial_distances(*blocks):
    return pl.pallas_call(
        partial_body,
        out_shape=jax.ShapeDtypeStruct((NF, 64, 128), jnp.bfloat16),
        in_specs=[pl.BlockSpec(memory_space=pl.ANY)] * 3,
        out_specs=pl.BlockSpec(memory_space=pltpu.VMEM),
        scratch_shapes=[
            pltpu.VMEM((7, ROWS, COLS), jnp.bfloat16),
            pltpu.SemaphoreType.DMA((7,)),
        ],
        compiler_params=pltpu.CompilerParams(vmem_limit_bytes=VMEM),
        cost_estimate=pl.CostEstimate(
            flops=2 * 24 * ROWS * ROWS * COLS, bytes_accessed=5 << 19, transcendentals=0
        ),
    )(*blocks)


def update_body(place, half, slots, both, out, xs, gs, arrived):
    copies = [
        [
            pltpu.make_async_copy(
                both.at[place[i] + kind], held.at[i * ROWS : (i + 1) * ROWS], arrived.at[kind, i]
            )
            for i in range(NZ * NC)
        ]
        for kind, held in enumerate((xs, gs))
    ]
    for copy in copies[0] + copies[1]:
        copy.start()
    blocks = []
    for k in range(NZ):
        blocks.append(jnp.concatenate([slots[4 * k], slots[4 * k + 2]], axis=0))
        blocks.append(jnp.concatenate([slots[4 * k + 1], slots[4 * k + 3]], axis=0))
    kernel = jnp.concatenate(blocks, axis=1)
    weight = jnp.sum(kernel.astype(jnp.float32), axis=1, keepdims=True)
    tiles = [slice(start, start + 256) for start in range(0, COLS, 256)]
    middle = NZ * NC // 2
    for copy in copies[0][:middle]:
        copy.wait()
    first, second = slice(0, middle * ROWS), slice(middle * ROWS, None)
    for at in tiles:
        spread = jnp.dot(kernel[:, first], xs[first, at], preferred_element_type=jnp.float32)
        out[:, at] = weight * xs[:ROWS, at].astype(jnp.float32) - spread
    for copy in copies[0][middle:]:
        copy.wait()
    for at in tiles:
        out[:, at] -= jnp.dot(kernel[:, second], xs[second, at], preferred_element_type=jnp.float32)
    for copy in copies[1]:
        copy.wait()
    for at in tiles:
        pulled = jnp.dot(kernel, gs[:, at], preferred_element_type=jnp.float32)
        out[:, at] = (half[0] * pulled + out[:, at]) / weight


def update(place, half, slots, both):
    return pl.pallas_call(
        update_body,
        out_shape=jax.ShapeDtypeStruct((ROWS, COLS), jnp.float32),
        in_specs=[
            pl.BlockSpec(memory_space=pltpu.SMEM),
            pl.BlockSpec(memory_space=pltpu.SMEM),
            pl.BlockSpec(memory_space=pltpu.VMEM),
            pl.BlockSpec(memory_space=pl.ANY),
        ],
        out_specs=pl.BlockSpec(memory_space=pltpu.VMEM),
        scratch_shapes=[
            pltpu.VMEM((2048, COLS), jnp.bfloat16),
            pltpu.VMEM((2048, COLS), jnp.bfloat16),
            pltpu.SemaphoreType.DMA((2, NZ * NC)),
        ],
        compiler_params=pltpu.CompilerParams(vmem_limit_bytes=VMEM),
        cost_estimate=pl.CostEstimate(
            flops=4 * ROWS * 2048 * COLS, bytes_accessed=10 << 20, transcendentals=0
        ),
    )(place, half, slots, both)


def homeward():
    pairs = []
    for z in range(NZ):
        for core in range(NC):
            for field in range(NF):
                chip = (z + (0, 0, 0, 0, -1, -1, 2, 2)[field // 4]) % NZ
                home = chip * NC + (core + field % 2) % NC
                pairs.append(((z * NC + core) * NF + field, home * NF + field))
    return pairs


def on_device(particles, gradients, kernel_scale):
    z, core = lax.axis_index("z"), lax.axis_index("core")
    index = np.arange(NZ * NC)
    chips = (z + np.array(OFFSETS, np.int32)[index // 2] + NZ) % NZ
    place = (4 * chips + 2 * ((core + index % 2) % 2)).astype(jnp.int32)
    half = 0.5 * kernel_scale
    own = jnp.concatenate([particles, gradients], axis=0)
    a1, a3 = shift(particles, 1), shift(particles, -2)
    a2 = shift(a1, 1)
    near = jnp.concatenate([particles, a1, a3], axis=0)
    near, a2, own, place, half, whole = lax.optimization_barrier(
        (near, a2, own, place, half, 2.0 * half)
    )
    both = lax.all_gather(own, DOM, axis=0, tiled=True)
    slots = partial_distances(near, other_core(near), a2)
    terms = lax.all_to_all(slots, FIELD, 0, 0, tiled=True)
    dist = jnp.maximum(jnp.sum(terms.astype(jnp.float32), axis=0), 0.0)
    piece = jnp.exp(-dist / whole[0]).astype(jnp.bfloat16)
    piece = lax.ppermute(piece, DOM + FIELD, homeward())
    pieces = lax.all_to_all(
        jnp.broadcast_to(piece[None], (NF, 64, 128)), FIELD, 0, 0, tiled=True
    )
    return update(place, half, pieces, both.reshape(2 * NZ * NC, ROWS, COLS))


def solution(mesh):
    fine = Mesh(mesh.devices.reshape(NZ, NC, NY, NX), DOM + FIELD)
    placed = (P(DOM, FIELD), P(DOM, FIELD), P())
    return jax.shard_map(
        on_device, mesh=fine, in_specs=placed, out_specs=P(DOM, FIELD), check_vma=False
    )
```

```python
import jax
import jax.numpy as jnp
import numpy as np
from jax import lax
from jax.experimental import pallas as pl
from jax.experimental.pallas import tpu as pltpu
from jax.sharding import Mesh, PartitionSpec as P

DOM = ("z", "core")
FIELD = ("y", "x")
NZ, NC, NY, NX = 8, 2, 8, 4
NF = NY * NX
ROWS, COLS = 128, 1024
VMEM = 48 * 1024 * 1024
OFFSETS = (0, -1, -2, 2, 1, 3, 4, -3)


def dot_rows(left, right):
    return lax.dot_general(
        left, right, (((1,), (1,)), ((), ())), preferred_element_type=jnp.float32
    )


def shift(array, hops):
    return lax.ppermute(array, "z", [(i, (i + hops) % NZ) for i in range(NZ)])


def other_core(array):
    return lax.ppermute(array, "core", [(0, 1), (1, 0)])


def partial_body(a, b, a2, out, held, arrived):
    rows = [pl.ds(i * ROWS, ROWS) for i in range(3)]
    sources = [ref.at[at] for at in rows for ref in (a, b)] + [a2]
    copies = [
        pltpu.make_async_copy(source, held.at[i], arrived.at[i])
        for i, source in enumerate(sources)
    ]
    for copy in copies:
        copy.start()
    for copy in copies:
        copy.wait()
    ones = jnp.ones((8, COLS), jnp.bfloat16)
    norms, lanes = {}, {}
    for i in range(7):
        wide = held[i].astype(jnp.float32)
        square = wide * wide
        if i < 6:
            norms[i] = jnp.sum(square, axis=1, keepdims=True)
        if i % 2 == 0:
            top = square.astype(jnp.bfloat16)
            rest = (square - top.astype(jnp.float32)).astype(jnp.bfloat16)
            lanes[i] = (dot_rows(ones, top) + dot_rows(ones, rest))[0:1]
    for first, pairs in (
        (0, ((0, 0), (1, 2), (2, 6), (3, 4))),
        (2, ((4, 0), (5, 4))),
        (4, ((6, 6), (7, 2))),
    ):
        for r in range(NC):
            for k, col in pairs:
                gram = dot_rows(held[first + r], held[col])
                part = (norms[first + r] + lanes[col] - 2.0 * gram).astype(jnp.bfloat16)
                out[4 * k + r] = part[:64]
                out[4 * k + 2 + r] = part[64:]


def partial_distances(*blocks):
    return pl.pallas_call(
        partial_body,
        out_shape=jax.ShapeDtypeStruct((NF, 64, 128), jnp.bfloat16),
        in_specs=[pl.BlockSpec(memory_space=pl.ANY)] * 3,
        out_specs=pl.BlockSpec(memory_space=pltpu.VMEM),
        scratch_shapes=[
            pltpu.VMEM((7, ROWS, COLS), jnp.bfloat16),
            pltpu.SemaphoreType.DMA((7,)),
        ],
        compiler_params=pltpu.CompilerParams(vmem_limit_bytes=VMEM),
        cost_estimate=pl.CostEstimate(
            flops=2 * 24 * ROWS * ROWS * COLS, bytes_accessed=5 << 19, transcendentals=0
        ),
    )(*blocks)


def update_body(place, half, slots, near, near_b, a2, both, out, xs, gs, arrived):
    here = {0: (near, 0), 1: (near_b, 0), 2: (near, 1), 3: (near_b, 1), 4: (a2, 0), 6: (near, 2), 7: (near_b, 2)}
    copies = [
        [
            pltpu.make_async_copy(
                both.at[place[i] + kind], held.at[i * ROWS : (i + 1) * ROWS], arrived.at[kind, i]
            )
            for i in range(NZ * NC)
            if kind == 1 or i not in here
        ]
        for kind, held in enumerate((xs, gs))
    ]
    for copy in copies[0] + copies[1]:
        copy.start()
    blocks = []
    for k in range(NZ):
        blocks.append(jnp.concatenate([slots[4 * k], slots[4 * k + 2]], axis=0))
        blocks.append(jnp.concatenate([slots[4 * k + 1], slots[4 * k + 3]], axis=0))
    kernel = jnp.concatenate(blocks, axis=1)
    weight = jnp.sum(kernel.astype(jnp.float32), axis=1, keepdims=True)
    tiles = [slice(start, start + 256) for start in range(0, COLS, 256)]
    for copy in copies[0]:
        copy.wait()

    def coords(at):
        parts = []
        for i in range(NZ * NC):
            ref, j = here.get(i, (xs, i))
            parts.append(ref[j * ROWS : (j + 1) * ROWS, at])
        return jnp.concatenate(parts, axis=0)

    for at in tiles:
        spread = jnp.dot(kernel, coords(at), preferred_element_type=jnp.float32)
        out[:, at] = weight * near[:ROWS, at].astype(jnp.float32) - spread
    for copy in copies[1]:
        copy.wait()
    for at in tiles:
        pulled = jnp.dot(kernel, gs[:, at], preferred_element_type=jnp.float32)
        out[:, at] = (half[0] * pulled + out[:, at]) / weight


def update(place, half, slots, near, near_b, a2, both):
    return pl.pallas_call(
        update_body,
        out_shape=jax.ShapeDtypeStruct((ROWS, COLS), jnp.float32),
        in_specs=[
            pl.BlockSpec(memory_space=pltpu.SMEM),
            pl.BlockSpec(memory_space=pltpu.SMEM),
            pl.BlockSpec(memory_space=pltpu.VMEM),
            pl.BlockSpec(memory_space=pltpu.VMEM),
            pl.BlockSpec(memory_space=pltpu.VMEM),
            pl.BlockSpec(memory_space=pltpu.VMEM),
            pl.BlockSpec(memory_space=pl.ANY),
        ],
        out_specs=pl.BlockSpec(memory_space=pltpu.VMEM),
        scratch_shapes=[
            pltpu.VMEM((2048, COLS), jnp.bfloat16),
            pltpu.VMEM((2048, COLS), jnp.bfloat16),
            pltpu.SemaphoreType.DMA((2, NZ * NC)),
        ],
        compiler_params=pltpu.CompilerParams(vmem_limit_bytes=VMEM),
        cost_estimate=pl.CostEstimate(
            flops=4 * ROWS * 2048 * COLS, bytes_accessed=10 << 20, transcendentals=0
        ),
    )(place, half, slots, near, near_b, a2, both)


def homeward():
    pairs = []
    for z in range(NZ):
        for core in range(NC):
            for field in range(NF):
                chip = (z + (0, 0, 0, 0, -1, -1, 2, 2)[field // 4]) % NZ
                home = chip * NC + (core + field % 2) % NC
                pairs.append(((z * NC + core) * NF + field, home * NF + field))
    return pairs


def on_device(particles, gradients, kernel_scale):
    z, core = lax.axis_index("z"), lax.axis_index("core")
    index = np.arange(NZ * NC)
    chips = (z + np.array(OFFSETS, np.int32)[index // 2] + NZ) % NZ
    place = (4 * chips + 2 * ((core + index % 2) % 2)).astype(jnp.int32)
    half = 0.5 * kernel_scale
    own = jnp.concatenate([particles, gradients], axis=0)
    a1, a3 = shift(particles, 1), shift(particles, -2)
    a2 = shift(a1, 1)
    near = jnp.concatenate([particles, a1, a3], axis=0)
    near, a2, own, place, half, whole = lax.optimization_barrier(
        (near, a2, own, place, half, 2.0 * half)
    )
    both = lax.all_gather(own, DOM, axis=0, tiled=True)
    near_b = other_core(near)
    slots = partial_distances(near, near_b, a2)
    terms = lax.all_to_all(slots, FIELD, 0, 0, tiled=True)
    dist = jnp.maximum(jnp.sum(terms.astype(jnp.float32), axis=0), 0.0)
    piece = jnp.exp(-dist / whole[0]).astype(jnp.bfloat16)
    piece = lax.ppermute(piece, DOM + FIELD, homeward())
    pieces = lax.all_to_all(
        jnp.broadcast_to(piece[None], (NF, 64, 128)), FIELD, 0, 0, tiled=True
    )
    return update(place, half, pieces, near, near_b, a2, both.reshape(2 * NZ * NC, ROWS, COLS))


def solution(mesh):
    fine = Mesh(mesh.devices.reshape(NZ, NC, NY, NX), DOM + FIELD)
    placed = (P(DOM, FIELD), P(DOM, FIELD), P())
    return jax.shard_map(
        on_device, mesh=fine, in_specs=placed, out_specs=P(DOM, FIELD), check_vma=False
    )
```

```python
import jax
import jax.numpy as jnp
import numpy as np
from jax import lax
from jax.experimental import pallas as pl
from jax.experimental.pallas import tpu as pltpu
from jax.sharding import Mesh, PartitionSpec as P

DOM = ("z", "core")
FIELD = ("y", "x")
NZ, NC, NY, NX = 8, 2, 8, 4
NF = NY * NX
ROWS, COLS = 128, 1024
VMEM = 48 * 1024 * 1024
OFFSETS = (0, -1, -2, 2, 1, 3, 4, -3)


def dot_rows(left, right):
    return lax.dot_general(
        left, right, (((1,), (1,)), ((), ())), preferred_element_type=jnp.float32
    )


def shift(array, hops):
    return lax.ppermute(array, "z", [(i, (i + hops) % NZ) for i in range(NZ)])


def other_core(array):
    return lax.ppermute(array, "core", [(0, 1), (1, 0)])


def partial_body(a, b, a2, out, held, arrived):
    rows = [pl.ds(i * ROWS, ROWS) for i in range(3)]
    sources = [ref.at[at] for at in rows for ref in (a, b)] + [a2]
    copies = [
        pltpu.make_async_copy(source, held.at[i], arrived.at[i])
        for i, source in enumerate(sources)
    ]
    for copy in copies:
        copy.start()
    for copy in copies:
        copy.wait()
    ones = jnp.ones((8, COLS), jnp.bfloat16)
    norms, lanes = {}, {}
    for i in range(7):
        wide = held[i].astype(jnp.float32)
        square = wide * wide
        if i < 6:
            norms[i] = jnp.sum(square, axis=1, keepdims=True)
        if i % 2 == 0:
            top = square.astype(jnp.bfloat16)
            rest = (square - top.astype(jnp.float32)).astype(jnp.bfloat16)
            lanes[i] = (dot_rows(ones, top) + dot_rows(ones, rest))[0:1]
    for first, pairs in (
        (0, ((0, 0), (1, 2), (2, 6), (3, 4))),
        (2, ((4, 0), (5, 4))),
        (4, ((6, 6), (7, 2))),
    ):
        for r in range(NC):
            for k, col in pairs:
                gram = dot_rows(held[first + r], held[col])
                part = (norms[first + r] + lanes[col] - 2.0 * gram).astype(jnp.bfloat16)
                out[4 * k + r] = part[:64]
                out[4 * k + 2 + r] = part[64:]


def partial_distances(*blocks):
    return pl.pallas_call(
        partial_body,
        out_shape=jax.ShapeDtypeStruct((NF, 64, 128), jnp.bfloat16),
        in_specs=[pl.BlockSpec(memory_space=pl.ANY)] * 3,
        out_specs=pl.BlockSpec(memory_space=pltpu.VMEM),
        scratch_shapes=[
            pltpu.VMEM((7, ROWS, COLS), jnp.bfloat16),
            pltpu.SemaphoreType.DMA((7,)),
        ],
        compiler_params=pltpu.CompilerParams(vmem_limit_bytes=VMEM),
        cost_estimate=pl.CostEstimate(
            flops=2 * 24 * ROWS * ROWS * COLS, bytes_accessed=5 << 19, transcendentals=0
        ),
    )(*blocks)


def update_body(place, half, slots, near, near_b, a2, both, out, xs, gs, arrived):
    here = {0: (near, 0), 1: (near_b, 0), 2: (near, 1), 3: (near_b, 1), 4: (a2, 0), 6: (near, 2), 7: (near_b, 2)}
    copies = [
        [
            pltpu.make_async_copy(
                both.at[place[i] + kind], held.at[i * ROWS : (i + 1) * ROWS], arrived.at[kind, i]
            )
            for i in range(NZ * NC)
            if kind == 1 or i not in here
        ]
        for kind, held in enumerate((xs, gs))
    ]
    for copy in copies[0] + copies[1]:
        copy.start()
    blocks = []
    for k in range(NZ):
        blocks.append(jnp.concatenate([slots[4 * k], slots[4 * k + 2]], axis=0))
        blocks.append(jnp.concatenate([slots[4 * k + 1], slots[4 * k + 3]], axis=0))
    kernel = jnp.concatenate(blocks, axis=1)
    weight = jnp.sum(kernel.astype(jnp.float32), axis=1, keepdims=True)
    tiles = [slice(start, start + 256) for start in range(0, COLS, 256)]
    for copy in copies[0]:
        copy.wait()

    def coords(at):
        parts = []
        for i in range(NZ * NC):
            ref, j = here.get(i, (xs, i))
            parts.append(ref[j * ROWS : (j + 1) * ROWS, at])
        return jnp.concatenate(parts, axis=0)

    for at in tiles:
        spread = jnp.dot(kernel, coords(at), preferred_element_type=jnp.float32)
        out[:, at] = weight * near[:ROWS, at].astype(jnp.float32) - spread
    for copy in copies[1]:
        copy.wait()
    for at in tiles:
        pulled = jnp.dot(kernel, gs[:, at], preferred_element_type=jnp.float32)
        out[:, at] = (half[0] * pulled + out[:, at]) / weight


def update(place, half, slots, near, near_b, a2, both):
    return pl.pallas_call(
        update_body,
        out_shape=jax.ShapeDtypeStruct((ROWS, COLS), jnp.float32),
        in_specs=[
            pl.BlockSpec(memory_space=pltpu.SMEM),
            pl.BlockSpec(memory_space=pltpu.SMEM),
            pl.BlockSpec(memory_space=pltpu.VMEM),
            pl.BlockSpec(memory_space=pltpu.VMEM),
            pl.BlockSpec(memory_space=pltpu.VMEM),
            pl.BlockSpec(memory_space=pltpu.VMEM),
            pl.BlockSpec(memory_space=pl.ANY),
        ],
        out_specs=pl.BlockSpec(memory_space=pltpu.VMEM),
        scratch_shapes=[
            pltpu.VMEM((2048, COLS), jnp.bfloat16),
            pltpu.VMEM((2048, COLS), jnp.bfloat16),
            pltpu.SemaphoreType.DMA((2, NZ * NC)),
        ],
        compiler_params=pltpu.CompilerParams(vmem_limit_bytes=VMEM),
        cost_estimate=pl.CostEstimate(
            flops=4 * ROWS * 2048 * COLS, bytes_accessed=10 << 20, transcendentals=0
        ),
    )(place, half, slots, near, near_b, a2, both)


def homeward():
    pairs = []
    for z in range(NZ):
        for core in range(NC):
            for field in range(NF):
                chip = (z + (0, 0, 0, 0, -1, -1, 2, 2)[field // 4]) % NZ
                home = chip * NC + (core + field % 2) % NC
                pairs.append(((z * NC + core) * NF + field, home * NF + field))
    return pairs


def on_device(particles, gradients, kernel_scale):
    z, core = lax.axis_index("z"), lax.axis_index("core")
    index = np.arange(NZ * NC)
    chips = (z + np.array(OFFSETS, np.int32)[index // 2] + NZ) % NZ
    place = (4 * chips + 2 * ((core + index % 2) % 2)).astype(jnp.int32)
    half = 0.5 * kernel_scale
    own = jnp.concatenate([particles, gradients], axis=0)
    a1, a3 = shift(particles, 1), shift(particles, -2)
    a2 = shift(a1, 1)
    near = jnp.concatenate([particles, a1, a3], axis=0)
    near_b = other_core(near)
    _, a2, own, place, half, whole = lax.optimization_barrier(
        (near, a2, own, place, half, 2.0 * half)
    )
    both = lax.all_gather(own, DOM, axis=0, tiled=True)
    slots = partial_distances(near, near_b, a2)
    terms = lax.all_to_all(slots, FIELD, 0, 0, tiled=True)
    dist = jnp.maximum(jnp.sum(terms.astype(jnp.float32), axis=0), 0.0)
    piece = jnp.exp(-dist / whole[0]).astype(jnp.bfloat16)
    piece = lax.ppermute(piece, DOM + FIELD, homeward())
    pieces = lax.all_to_all(
        jnp.broadcast_to(piece[None], (NF, 64, 128)), FIELD, 0, 0, tiled=True
    )
    return update(place, half, pieces, near, near_b, a2, both.reshape(2 * NZ * NC, ROWS, COLS))


def solution(mesh):
    fine = Mesh(mesh.devices.reshape(NZ, NC, NY, NX), DOM + FIELD)
    placed = (P(DOM, FIELD), P(DOM, FIELD), P())
    return jax.shard_map(
        on_device, mesh=fine, in_specs=placed, out_specs=P(DOM, FIELD), check_vma=False
    )
```

```python
import jax
import jax.numpy as jnp
import numpy as np
from jax import lax
from jax.experimental import pallas as pl
from jax.experimental.pallas import tpu as pltpu
from jax.sharding import Mesh, PartitionSpec as P

DOM = ("z", "core")
FIELD = ("y", "x")
NZ, NC, NY, NX = 8, 2, 8, 4
NF = NY * NX
ROWS, COLS = 128, 1024
VMEM = 48 * 1024 * 1024
OFFSETS = (0, -1, -2, 2, 1, 3, 4, -3)


def dot_rows(left, right):
    return lax.dot_general(
        left, right, (((1,), (1,)), ((), ())), preferred_element_type=jnp.float32
    )


def shift(array, hops):
    return lax.ppermute(array, "z", [(i, (i + hops) % NZ) for i in range(NZ)])


def other_core(array):
    return lax.ppermute(array, "core", [(0, 1), (1, 0)])


def partial_body(a, b, a2, out, held, arrived):
    rows = [pl.ds(i * ROWS, ROWS) for i in range(3)]
    sources = [ref.at[at] for at in rows for ref in (a, b)] + [a2]
    copies = [
        pltpu.make_async_copy(source, held.at[i], arrived.at[i])
        for i, source in enumerate(sources)
    ]
    for copy in copies:
        copy.start()
    for copy in copies:
        copy.wait()
    ones = jnp.ones((8, COLS), jnp.bfloat16)
    norms, lanes = {}, {}
    for i in range(7):
        wide = held[i].astype(jnp.float32)
        square = wide * wide
        if i < 6:
            norms[i] = jnp.sum(square, axis=1, keepdims=True)
        if i % 2 == 0:
            top = square.astype(jnp.bfloat16)
            rest = (square - top.astype(jnp.float32)).astype(jnp.bfloat16)
            lanes[i] = (dot_rows(ones, top) + dot_rows(ones, rest))[0:1]
    for first, pairs in (
        (0, ((0, 0), (1, 2), (2, 6), (3, 4))),
        (2, ((4, 0), (5, 4))),
        (4, ((6, 6), (7, 2))),
    ):
        for r in range(NC):
            for k, col in pairs:
                gram = dot_rows(held[first + r], held[col])
                part = (norms[first + r] + lanes[col] - 2.0 * gram).astype(jnp.bfloat16)
                out[4 * k + r] = part[:64]
                out[4 * k + 2 + r] = part[64:]


def partial_distances(*blocks):
    return pl.pallas_call(
        partial_body,
        out_shape=jax.ShapeDtypeStruct((NF, 64, 128), jnp.bfloat16),
        in_specs=[pl.BlockSpec(memory_space=pl.ANY)] * 3,
        out_specs=pl.BlockSpec(memory_space=pltpu.VMEM),
        scratch_shapes=[
            pltpu.VMEM((7, ROWS, COLS), jnp.bfloat16),
            pltpu.SemaphoreType.DMA((7,)),
        ],
        compiler_params=pltpu.CompilerParams(vmem_limit_bytes=VMEM),
        cost_estimate=pl.CostEstimate(
            flops=2 * 24 * ROWS * ROWS * COLS, bytes_accessed=5 << 19, transcendentals=0
        ),
    )(*blocks)


def update_body(place, half, slots, near, near_b, a2, both, out, xs, gs, arrived):
    here = {0: (near, 0), 1: (near_b, 0), 2: (near, 1), 3: (near_b, 1), 4: (a2, 0), 6: (near, 2), 7: (near_b, 2)}
    copies = [
        [
            pltpu.make_async_copy(
                both.at[place[i] + kind], held.at[i * ROWS : (i + 1) * ROWS], arrived.at[kind, i]
            )
            for i in range(NZ * NC)
            if kind == 1 or i not in here
        ]
        for kind, held in enumerate((xs, gs))
    ]
    for copy in copies[0] + copies[1]:
        copy.start()
    blocks = []
    for k in range(NZ):
        blocks.append(jnp.concatenate([slots[4 * k], slots[4 * k + 2]], axis=0))
        blocks.append(jnp.concatenate([slots[4 * k + 1], slots[4 * k + 3]], axis=0))
    kernel = jnp.concatenate(blocks, axis=1)
    weight = jnp.sum(kernel.astype(jnp.float32), axis=1, keepdims=True)
    tiles = [slice(start, start + 256) for start in range(0, COLS, 256)]
    away = [i for i in range(NZ * NC) if i not in here]
    for_here = jnp.concatenate([blocks[i] for i in here], axis=1)
    for_away = jnp.concatenate([blocks[i] for i in away], axis=1)
    for at in tiles:
        held = [ref[j * ROWS : (j + 1) * ROWS, at] for ref, j in here.values()]
        spread = jnp.dot(
            for_here, jnp.concatenate(held, axis=0), preferred_element_type=jnp.float32
        )
        out[:, at] = weight * near[:ROWS, at].astype(jnp.float32) - spread
    for copy in copies[0]:
        copy.wait()
    for at in tiles:
        held = [xs[i * ROWS : (i + 1) * ROWS, at] for i in away]
        out[:, at] -= jnp.dot(
            for_away, jnp.concatenate(held, axis=0), preferred_element_type=jnp.float32
        )
    for copy in copies[1]:
        copy.wait()
    for at in tiles:
        pulled = jnp.dot(kernel, gs[:, at], preferred_element_type=jnp.float32)
        out[:, at] = (half[0] * pulled + out[:, at]) / weight


def update(place, half, slots, near, near_b, a2, both):
    return pl.pallas_call(
        update_body,
        out_shape=jax.ShapeDtypeStruct((ROWS, COLS), jnp.float32),
        in_specs=[
            pl.BlockSpec(memory_space=pltpu.SMEM),
            pl.BlockSpec(memory_space=pltpu.SMEM),
            pl.BlockSpec(memory_space=pltpu.VMEM),
            pl.BlockSpec(memory_space=pltpu.VMEM),
            pl.BlockSpec(memory_space=pltpu.VMEM),
            pl.BlockSpec(memory_space=pltpu.VMEM),
            pl.BlockSpec(memory_space=pl.ANY),
        ],
        out_specs=pl.BlockSpec(memory_space=pltpu.VMEM),
        scratch_shapes=[
            pltpu.VMEM((2048, COLS), jnp.bfloat16),
            pltpu.VMEM((2048, COLS), jnp.bfloat16),
            pltpu.SemaphoreType.DMA((2, NZ * NC)),
        ],
        compiler_params=pltpu.CompilerParams(vmem_limit_bytes=VMEM),
        cost_estimate=pl.CostEstimate(
            flops=4 * ROWS * 2048 * COLS, bytes_accessed=10 << 20, transcendentals=0
        ),
    )(place, half, slots, near, near_b, a2, both)


def homeward():
    pairs = []
    for z in range(NZ):
        for core in range(NC):
            for field in range(NF):
                chip = (z + (0, 0, 0, 0, -1, -1, 2, 2)[field // 4]) % NZ
                home = chip * NC + (core + field % 2) % NC
                pairs.append(((z * NC + core) * NF + field, home * NF + field))
    return pairs


def on_device(particles, gradients, kernel_scale):
    z, core = lax.axis_index("z"), lax.axis_index("core")
    index = np.arange(NZ * NC)
    chips = (z + np.array(OFFSETS, np.int32)[index // 2] + NZ) % NZ
    place = (4 * chips + 2 * ((core + index % 2) % 2)).astype(jnp.int32)
    half = 0.5 * kernel_scale
    own = jnp.concatenate([particles, gradients], axis=0)
    a1, a3 = shift(particles, 1), shift(particles, -2)
    a2 = shift(a1, 1)
    near = jnp.concatenate([particles, a1, a3], axis=0)
    near, a2, own, place, half, whole = lax.optimization_barrier(
        (near, a2, own, place, half, 2.0 * half)
    )
    both = lax.all_gather(own, DOM, axis=0, tiled=True)
    near_b = other_core(near)
    slots = partial_distances(near, near_b, a2)
    terms = lax.all_to_all(slots, FIELD, 0, 0, tiled=True)
    dist = jnp.maximum(jnp.sum(terms.astype(jnp.float32), axis=0), 0.0)
    piece = jnp.exp(-dist / whole[0]).astype(jnp.bfloat16)
    piece = lax.ppermute(piece, DOM + FIELD, homeward())
    pieces = lax.all_to_all(
        jnp.broadcast_to(piece[None], (NF, 64, 128)), FIELD, 0, 0, tiled=True
    )
    return update(place, half, pieces, near, near_b, a2, both.reshape(2 * NZ * NC, ROWS, COLS))


def solution(mesh):
    fine = Mesh(mesh.devices.reshape(NZ, NC, NY, NX), DOM + FIELD)
    placed = (P(DOM, FIELD), P(DOM, FIELD), P())
    return jax.shard_map(
        on_device, mesh=fine, in_specs=placed, out_specs=P(DOM, FIELD), check_vma=False
    )
```
